32 devices in a mesh: row: 16 (over z, y, x), col: 2 (over core).
Axes of the slice: x: 2, y: 2, z: 4, core: 2. Of those that a mesh axis runs over, the one named last changes fastest.
Arguments:
- current: bfloat16 [2, 64, 8, 4, 128], P(None, 'row', 'col'), may hold values from -6 to 6
- probe: bfloat16 [2, 64, 8, 4, 128], P(None, 'row', 'col'), may hold values from -6 to 6
- near_list: int32 [64, 8, 2], P('row', 'col'), may hold values from 0 to 9, as said below
- near_blocks: bfloat16 [2, 64, 8, 2, 128, 128], P(None, 'row', 'col'), may hold values from -0.25 to 0.25
- radiation: bfloat16 [2, 128, 128], replicated, may hold values from -0.375 to 0.375
- reception: bfloat16 [2, 128, 128], replicated, may hold values from -0.375 to 0.375
- interp: float32 [256, 128], replicated, may hold values from -0.5 to 0.5
- phase: float32 [16, 256], replicated, may hold values from -3.140625 to 3.140625
- leaf_table: float32 [2, 15, 15, 128], replicated, may hold values from -0.36 to 0.36
- coarse_table: bfloat16 [2, 31, 3, 256], replicated, may hold values from -0.023925781 to 0.023925781
Outputs:
- forward_out: float32 [2, 64, 8, 4, 128], P(None, 'row', 'col')
- adjoint_out: float32 [2, 64, 8, 4, 128], P(None, 'row', 'col')
The draws below stay inside these ranges and needn't reach their ends.
Inputs may be any that keep to these rules, and one draw needn't show every extreme that they name: `near_list`: the 2 slots of a box hold distinct codes; only slots after the first may be empty (code 9).
All inputs are finite; a program needn't handle non-finite values.
Results may differ from the reference program's by a relative error of at most 0.0027.
Values may be sent and summed in bfloat16 or wider, within the bound.
A program may use at most 128 MiB of HBM per device.

```python
import jax
import jax.numpy as jnp
from jax import lax

P_SIZE = 128
Q0 = 128
Q1 = 256
K = 2
SIDE = 4
RHS = 4
NR = 64
NC = 8
OFFS = 15
TROWS = 31
TCOLS = 3
N_ROW = 16
N_COL = 2


def draw_near_list(key, part):
    key_order = jax.random.fold_in(key, 11)
    key_empty = jax.random.fold_in(key, 12)
    scores = jax.random.randint(key_order, (NR, NC, 9), 0, 2 ** 20) * 16 + jnp.arange(9, dtype=jnp.int32)
    ranked = jnp.argsort(scores, axis=-1, stable=True)[..., :K].astype(jnp.int32)
    empty_slot = jax.random.randint(key_empty, (NR, NC, K), 0, 4) == 0
    slot_index = jnp.arange(K, dtype=jnp.int32)
    empty_slot = empty_slot & (slot_index > 0)
    return jnp.where(empty_slot, 9, ranked).astype(jnp.int32)


def level_of(rng, extent, split, least, top_value):
    gain = 1.0
    for axis_at, blocks in split:
        heights = jax.random.uniform(jax.random.fold_in(jax.random.fold_in(rng, 6), axis_at), (blocks,), jnp.float32, least / len(split), top_value / len(split))
        gain = gain * jnp.repeat(jnp.exp(heights), extent[axis_at] // blocks).reshape((-1,) + (1,) * (len(extent) - 1 - axis_at))
    return gain


def bell_draw(stream_key, extent, scale, limit, shards=(), kind=jnp.bfloat16):
    result = jax.random.normal(stream_key, extent, jnp.float32) * scale
    if len(shards) > 0:
        result = level_of(stream_key, extent, shards, -0.22, 0.18) * result
    return jnp.clip(result, min=-limit, max=limit).astype(kind)


def setup_inputs(seed: int = 0) -> dict:
    streams_of = jax.random.split(jax.random.key(seed), 11)
    current = bell_draw(streams_of[0], (2, NR, NC, RHS, P_SIZE), 1.0, 6.0, ((1, 16), (2, 2)))
    probe = bell_draw(streams_of[1], (2, NR, NC, RHS, P_SIZE), 1.0, 6.0, ((1, 16), (2, 2)))
    near_list = draw_near_list(jax.random.fold_in(streams_of[10], 71), 0)
    near_blocks = bell_draw(streams_of[3], (2, NR, NC, K, P_SIZE, P_SIZE), (2 * K * P_SIZE) ** -0.5, 0.25, ((1, 16), (2, 2)))
    radiation = bell_draw(streams_of[4], (2, Q0, P_SIZE), (2 * P_SIZE) ** -0.5, 0.375)
    reception = bell_draw(streams_of[5], (2, P_SIZE, Q0), (2 * Q0) ** -0.5, 0.375)
    interp = bell_draw(streams_of[6], (Q1, Q0), Q0 ** -0.5, 0.5, (), jnp.float32)
    phase = jnp.clip(jax.random.uniform(streams_of[7], (SIDE * SIDE, Q1), jnp.float32, -3.140625, 3.140625), -3.140625, 3.140625)
    leaf_table = bell_draw(streams_of[8], (2, OFFS, OFFS, Q0), 0.06, 0.36, (), jnp.float32)
    coarse_table = bell_draw(streams_of[9], (2, TROWS, TCOLS, Q1), 0.004, 0.023925781)
    return dict(current=current, probe=probe, near_list=near_list, near_blocks=near_blocks, radiation=radiation, reception=reception, interp=interp, phase=phase, leaf_table=leaf_table, coarse_table=coarse_table)


HIGH = lax.Precision.HIGHEST


def complex_mul(left_re, left_im, right_re, right_im):
    return left_re * right_re - left_im * right_im, left_re * right_im + left_im * right_re


def conj_flip(table, axes):
    flipped = jnp.flip(table, axes)
    return jnp.stack([flipped[0], -flipped[1]])


def near_part(current, probe, near_list, near_blocks):
    pad_cur = jnp.pad(current.astype(jnp.float32), ((0, 0), (1, 1), (1, 1), (0, 0), (0, 0)))

    def one_row(row_index):
        row_index = row_index.astype(jnp.int32)
        blocks = lax.dynamic_index_in_dim(near_blocks, row_index, 1, keepdims=False).astype(jnp.float32)
        slot_codes = lax.dynamic_index_in_dim(near_list, row_index, 0, keepdims=False)
        band = lax.dynamic_slice_in_dim(pad_cur, row_index, 3, 1)
        shifted = jnp.stack([band[:, offset_code // 3, offset_code % 3:offset_code % 3 + NC] for offset_code in range(9)])
        one_hot = (slot_codes[..., None] == jnp.arange(9, dtype=jnp.int32)).astype(jnp.float32)
        picked = jnp.einsum('cko,oxcmp->xkcmp', one_hot, shifted, precision=HIGH)
        blocks_re, blocks_im = blocks[0], blocks[1]
        fwd_re = jnp.einsum('ckpq,kcmq->cmp', blocks_re, picked[0], precision=HIGH) - jnp.einsum('ckpq,kcmq->cmp', blocks_im, picked[1], precision=HIGH)
        fwd_im = jnp.einsum('ckpq,kcmq->cmp', blocks_re, picked[1], precision=HIGH) + jnp.einsum('ckpq,kcmq->cmp', blocks_im, picked[0], precision=HIGH)
        probe_row = lax.dynamic_index_in_dim(probe, row_index, 1, keepdims=False).astype(jnp.float32)
        back_re = jnp.einsum('ckpq,cmp->kcmq', blocks_re, probe_row[0], precision=HIGH) + jnp.einsum('ckpq,cmp->kcmq', blocks_im, probe_row[1], precision=HIGH)
        back_im = jnp.einsum('ckpq,cmp->kcmq', blocks_re, probe_row[1], precision=HIGH) - jnp.einsum('ckpq,cmp->kcmq', blocks_im, probe_row[0], precision=HIGH)
        return jnp.stack([fwd_re, fwd_im]), jnp.stack([back_re, back_im])

    fwd_rows, contrib = lax.map(one_row, jnp.arange(NR, dtype=jnp.int32))
    near_fwd = jnp.moveaxis(fwd_rows, 0, 1)
    contrib = jnp.moveaxis(contrib, 0, 2)
    placed = jnp.zeros((2, NR + 2, NC + 2, RHS, P_SIZE), jnp.float32)
    for offset_code in range(9):
        mask_code = (near_list == offset_code).astype(jnp.float32)
        selected = jnp.einsum('rck,xkrcmp->xrcmp', mask_code, contrib, precision=HIGH)
        placed = placed.at[:, offset_code // 3:offset_code // 3 + NR, offset_code % 3:offset_code % 3 + NC].add(selected)
    near_adj = placed[:, 1:NR + 1, 1:NC + 1]
    return near_fwd, near_adj


def far_part(vector, rad_re, rad_im, rcv_re, rcv_im, leaf_table, coarse_table, interp, phase):
    values = vector.astype(jnp.float32)
    rad_re = rad_re.astype(jnp.float32)
    rad_im = rad_im.astype(jnp.float32)
    out_re = jnp.einsum('rcmp,qp->rcmq', values[0], rad_re, precision=HIGH) - jnp.einsum('rcmp,qp->rcmq', values[1], rad_im, precision=HIGH)
    out_im = jnp.einsum('rcmp,qp->rcmq', values[0], rad_im, precision=HIGH) + jnp.einsum('rcmp,qp->rcmq', values[1], rad_re, precision=HIGH)
    reach = 2 * SIDE - 1
    pad_re = jnp.pad(out_re, ((reach, reach), (reach, reach), (0, 0), (0, 0)))
    pad_im = jnp.pad(out_im, ((reach, reach), (reach, reach), (0, 0), (0, 0)))
    row_ids = jnp.arange(NR, dtype=jnp.int32)
    col_ids = jnp.arange(NC, dtype=jnp.int32)

    def leaf_step(index, carry):
        acc_re, acc_im = carry
        index = index.astype(jnp.int32)
        row_off = index // OFFS - reach
        col_off = index % OFFS - reach
        start_row = (reach + row_off).astype(jnp.int32)
        start_col = (reach + col_off).astype(jnp.int32)
        zero = jnp.zeros((), jnp.int32)
        src_re = lax.dynamic_slice(pad_re, (start_row, start_col, zero, zero), (NR, NC, RHS, Q0))
        src_im = lax.dynamic_slice(pad_im, (start_row, start_col, zero, zero), (NR, NC, RHS, Q0))
        ok_rows = jnp.abs((row_ids + row_off) // SIDE - row_ids // SIDE) <= 1
        ok_cols = jnp.abs((col_ids + col_off) // SIDE - col_ids // SIDE) <= 1
        adjacent = (jnp.abs(row_off) <= 1) & (jnp.abs(col_off) <= 1)
        valid = (ok_rows[:, None] & ok_cols[None, :] & jnp.logical_not(adjacent)).astype(jnp.float32)
        coeff = lax.dynamic_slice(leaf_table, (zero, (index // OFFS).astype(jnp.int32), (index % OFFS).astype(jnp.int32), zero), (2, 1, 1, Q0)).reshape(2, Q0)
        part_re, part_im = complex_mul(coeff[0], coeff[1], src_re, src_im)
        return acc_re + part_re * valid[:, :, None, None], acc_im + part_im * valid[:, :, None, None]

    zeros_leaf = jnp.zeros((NR, NC, RHS, Q0), jnp.float32)
    leaf_re, leaf_im = lax.fori_loop(0, OFFS * OFFS, leaf_step, (zeros_leaf, zeros_leaf))

    interp_re = jnp.einsum('kq,rcmq->rcmk', interp, out_re, precision=HIGH).reshape(N_ROW, SIDE, N_COL, SIDE, RHS, Q1)
    interp_im = jnp.einsum('kq,rcmq->rcmk', interp, out_im, precision=HIGH).reshape(N_ROW, SIDE, N_COL, SIDE, RHS, Q1)
    angles = phase.reshape(SIDE, SIDE, Q1)
    cos_ph = jnp.cos(angles)[None, :, None, :, None, :]
    sin_ph = jnp.sin(angles)[None, :, None, :, None, :]
    top_re = jnp.sum(cos_ph * interp_re - sin_ph * interp_im, axis=(1, 3))
    top_im = jnp.sum(cos_ph * interp_im + sin_ph * interp_re, axis=(1, 3))
    top_b = jnp.stack([top_re, top_im]).astype(jnp.bfloat16)
    top_f = lax.optimization_barrier(top_b).astype(jnp.float32)

    table_f = coarse_table.astype(jnp.float32)
    col_index = jnp.arange(N_COL, dtype=jnp.int32)
    col_diff = col_index[:, None] - col_index[None, :]
    row_index_all = jnp.arange(N_ROW, dtype=jnp.int32)

    def one_target(target_row):
        target_row = target_row.astype(jnp.int32)
        row_pick = jnp.take(table_f, target_row - row_index_all + N_ROW - 1, axis=1)
        joint = row_pick[:, :, col_diff + N_COL - 1]
        distant = (jnp.abs(target_row - row_index_all)[:, None, None] > 1) | (jnp.abs(col_diff)[None] > 1)
        weight = distant.astype(jnp.float32)[..., None]
        joint_re = joint[0] * weight
        joint_im = joint[1] * weight
        got_re = jnp.einsum('scdq,sdmq->cmq', joint_re, top_f[0], precision=HIGH) - jnp.einsum('scdq,sdmq->cmq', joint_im, top_f[1], precision=HIGH)
        got_im = jnp.einsum('scdq,sdmq->cmq', joint_re, top_f[1], precision=HIGH) + jnp.einsum('scdq,sdmq->cmq', joint_im, top_f[0], precision=HIGH)
        return jnp.stack([got_re, got_im])

    coarse_in = jnp.moveaxis(lax.map(one_target, row_index_all), 0, 1)
    in_re = coarse_in[0][:, None, :, None]
    in_im = coarse_in[1][:, None, :, None]
    back_re = (cos_ph * in_re + sin_ph * in_im).reshape(NR, NC, RHS, Q1)
    back_im = (cos_ph * in_im - sin_ph * in_re).reshape(NR, NC, RHS, Q1)
    spread_re = jnp.einsum('kq,rcmk->rcmq', interp, back_re, precision=HIGH)
    spread_im = jnp.einsum('kq,rcmk->rcmq', interp, back_im, precision=HIGH)
    incoming = jnp.stack([leaf_re + spread_re, leaf_im + spread_im]).astype(jnp.bfloat16)
    incoming = lax.optimization_barrier(incoming).astype(jnp.float32)
    rcv_re = rcv_re.astype(jnp.float32)
    rcv_im = rcv_im.astype(jnp.float32)
    res_re = jnp.einsum('rcmq,pq->rcmp', incoming[0], rcv_re, precision=HIGH) - jnp.einsum('rcmq,pq->rcmp', incoming[1], rcv_im, precision=HIGH)
    res_im = jnp.einsum('rcmq,pq->rcmp', incoming[0], rcv_im, precision=HIGH) + jnp.einsum('rcmq,pq->rcmp', incoming[1], rcv_re, precision=HIGH)
    return jnp.stack([res_re, res_im])


def reference(current, probe, near_list, near_blocks, radiation, reception, interp, phase, leaf_table, coarse_table):
    near_fwd, near_adj = near_part(current, probe, near_list, near_blocks)
    far_fwd = far_part(current, radiation[0], radiation[1], reception[0], reception[1], leaf_table, coarse_table, interp, phase)
    far_adj = far_part(probe, reception[0].T, -reception[1].T, radiation[0].T, -radiation[1].T, conj_flip(leaf_table, (1, 2)), conj_flip(coarse_table, (1, 2)), interp, phase)
    return near_fwd + far_fwd, near_adj + far_adj
```

```python
import functools

import jax
import jax.numpy as jnp
from jax import lax
from jax.experimental import pallas as pl
from jax.experimental.pallas import tpu as pltpu
from jax.sharding import PartitionSpec as P

HIGH = lax.Precision.HIGHEST
F32 = jnp.float32
BF16 = jnp.bfloat16
MESH = pl.DeviceIdType.MESH


def upper(shape):
    return lax.broadcasted_iota(jnp.int32, shape, len(shape) - 2) < 4


def swap(x):
    turned = pltpu.roll(x, 4, x.ndim - 2)
    return jnp.where(upper(x.shape), -turned, turned)


def interleave(re, im):
    low = upper(re.shape)
    return jnp.where(low, re, pltpu.roll(im, 4, 1)), jnp.where(low, pltpu.roll(re, 4, 1), im)


def nn(a, b, precision=None):
    return lax.dot_general(a, b, (((1,), (0,)), ((), ())), precision=precision, preferred_element_type=F32)


def nt(a, b, precision=None):
    return lax.dot_general(a, b, (((1,), (1,)), ((), ())), precision=precision, preferred_element_type=F32)


def kernel(
    n_row,
    n_col,
    cur,
    prb,
    codes,
    near_hbm,
    rad,
    rec,
    interp,
    phase,
    leaf_tab,
    coarse_tab,
    out_fwd,
    out_adj,
    halo,
    gath,
    near,
    w_rad,
    w_rcv,
    tab,
    patt,
    leaf,
    vec,
    window,
    placed,
    ring_out,
    ring_in,
    near_fwd,
    back,
    trig,
    near_sem,
    halo_send,
    halo_recv,
    ring_send,
    ring_recv,
    all_send,
    all_recv,
):
    row = lax.axis_index("row")
    col = lax.axis_index("col")
    total = n_row * n_col
    me = row * n_col + col

    barrier = pltpu.get_barrier_semaphore()

    def greet(n, carry):
        @pl.when(n != me)
        def _():
            pl.semaphore_signal(barrier, inc=1, device_id=(n // n_col, n % n_col), device_id_type=MESH)

        return carry

    lax.fori_loop(0, total, greet, 0)
    load_near = pltpu.make_async_copy(near_hbm, near, near_sem)
    load_near.start()

    halo[4, 0:128] = cur[...]
    halo[4, 128:256] = prb[...]
    for x in range(2):
        sign = 1.0 if x == 0 else -1.0
        cols = slice(128 * x, 128 * x + 128)
        rad_f = rad[x].astype(F32)
        rec_f = rec[x].astype(F32)
        w_rad[0, :, cols] = rad_f.T.astype(BF16)
        w_rad[1, :, cols] = (rec_f * sign).astype(BF16)
        w_rcv[0, :, cols] = rec_f.T.astype(BF16)
        w_rcv[1, :, cols] = (rad_f * sign).astype(BF16)
    angles = phase[...]
    trig[0] = jnp.cos(angles)
    trig[1] = jnp.sin(angles)

    def patterns(slot):
        for s in range(2):
            both = nn(halo[slot, 128 * s : 128 * s + 128], w_rad[s])
            re = (both[:64, :128] - both[64:, 128:]).reshape(8, 8, 128)
            im = (both[64:, :128] + both[:64, 128:]).reshape(8, 8, 128)
            even, odd = interleave(re, im)
            patt[s, 0, :, 0] = even
            patt[s, 0, :, 1] = odd
            patt[s, 1, :, 0] = swap(even) if s == 0 else -swap(even)
            patt[s, 1, :, 1] = swap(odd) if s == 0 else -swap(odd)

    def boxes_of(slot, s):
        base = 128 * s
        re = halo[slot, base : base + 64].astype(F32).reshape(8, 8, 128)
        im = halo[slot, base + 64 : base + 128].astype(F32).reshape(8, 8, 128)
        return interleave(re, im)

    patterns(4)
    for s in range(2):
        own = patt[s, 0].reshape(128, 128)
        wide = nt(own, interp[...], HIGH).reshape(16, 8, 256)
        cos_sum = jnp.zeros((8, 256), F32)
        sin_sum = jnp.zeros((8, 256), F32)
        for j in range(16):
            cos_sum += trig[0, j : j + 1] * wide[j]
            sin_sum += trig[1, j : j + 1] * wide[j]
        top = cos_sum + swap(sin_sum)
        vec[0, s] = top
    gath[me] = vec[0].reshape(16, 256).astype(BF16)

    pl.semaphore_wait(barrier, total - 1)

    def halo_copy(d):
        dr = d // 3 - 1
        dc = d % 3 - 1
        return pltpu.make_async_remote_copy(
            src_ref=halo.at[4],
            dst_ref=halo.at[8 - d],
            send_sem=halo_send.at[d],
            recv_sem=halo_recv.at[8 - d],
            device_id=(row + dr, col + dc),
            device_id_type=MESH,
        )

    def exists(d):
        r = row + d // 3 - 1
        c = col + d % 3 - 1
        return (d != 4) & (r >= 0) & (r < n_row) & (c >= 0) & (c < n_col)

    def send_halo(d, carry):
        @pl.when(exists(d))
        def _():
            halo_copy(d).start()

        return carry

    lax.fori_loop(0, 9, send_halo, 0)

    def send_top(n, carry):
        @pl.when(n != me)
        def _():
            pltpu.make_async_remote_copy(
                src_ref=gath.at[me],
                dst_ref=gath.at[me],
                send_sem=all_send,
                recv_sem=all_recv,
                device_id=(n // n_col, n % n_col),
                device_id_type=MESH,
            ).start()

        return carry

    lax.fori_loop(0, total, send_top, 0)

    window[...] = jnp.zeros_like(window)
    placed[...] = jnp.zeros_like(placed)
    even, odd = boxes_of(4, 0)
    for b in range(16):
        window[(b // 4 + 1) * 6 + b % 4 + 1] = (odd if b % 2 else even)[b // 2]
    even, odd = boxes_of(4, 1)
    back[:, 0] = even
    back[:, 1] = odd
    load_near.wait()

    def adjoint_row(r, carry):
        for c in range(4):
            y = back[r * 2 + c // 2, c % 2].astype(BF16)
            parts = []
            for k in range(2):
                a = nn(y, near[0, r * 4 + c, k])
                b = nn(y, near[1, r * 4 + c, k])
                parts.append(a - swap(b))
            for o in range(9):
                place = (r + o // 3) * 6 + c + o % 3
                term = placed[place]
                for k in range(2):
                    term += jnp.where(codes[r, c, k] == o, 1.0, 0.0) * parts[k]
                placed[place] = term
        return carry

    lax.fori_loop(0, 4, adjoint_row, 0)

    def span(step):
        return {-1: [0], 0: [1, 2, 3, 4], 1: [5]}[step]

    def ring_copy(d):
        dr, dc = d // 3 - 1, d % 3 - 1
        size = 4 if dr == 0 or dc == 0 else 1
        return pltpu.make_async_remote_copy(
            src_ref=ring_out.at[d, pl.ds(0, size)],
            dst_ref=ring_in.at[8 - d, pl.ds(0, size)],
            send_sem=ring_send.at[d],
            recv_sem=ring_recv.at[8 - d],
            device_id=(row + dr, col + dc),
            device_id_type=MESH,
        )

    directions = [d for d in range(9) if d != 4]
    for d in directions:

        @pl.when(exists(d))
        def _(d=d):
            at = 0
            for r in span(d // 3 - 1):
                for c in span(d % 3 - 1):
                    ring_out[d, at] = placed[r * 6 + c]
                    at += 1
            ring_copy(d).start()

    def spread_table(jr, carry):
        for x in range(2):
            rows = leaf_tab[x, jr]
            for jc in range(15):
                tab[x, jr * 15 + jc] = jnp.broadcast_to(rows[jc : jc + 1], (8, 128))
        return carry

    lax.fori_loop(0, 15, spread_table, 0)
    for x in range(2):
        for jr in range(6, 9):
            for jc in range(6, 9):
                tab[x, jr * 15 + jc] = jnp.zeros((8, 128), F32)
    leaf[...] = jnp.zeros_like(leaf)

    def translate(br, bc):
        for s in range(2):

            def source_row(rr, acc, s=s):
                acc = list(acc)
                plain = [patt[s, 0, rr * 2 + cc // 2, cc % 2] for cc in range(4)]
                turned = [patt[s, 1, rr * 2 + cc // 2, cc % 2] for cc in range(4)]
                for r in range(4):
                    for dc in range(-3, 4):
                        at = (br * 4 + rr + 3 - r) * 15 + bc * 4 + dc + 3
                        if s == 1:
                            at = 224 - at
                        t_re = tab[0, at]
                        t_im = tab[1, at]
                        for c in range(4):
                            cc = c + dc
                            if 0 <= cc < 4:
                                acc[r * 4 + c] += t_re * plain[cc] + t_im * turned[cc]
                return tuple(acc)

            acc = lax.fori_loop(0, 4, source_row, tuple(leaf[s, b] for b in range(16)))
            for b in range(16):
                leaf[s, b] = acc[b]

    translate(1, 1)

    def side_block(d, carry):
        @pl.when(exists(d))
        def _():
            halo_copy(8 - d).wait_recv()
            patterns(d)
            translate(d // 3, d % 3)

        return carry

    lax.fori_loop(0, 9, side_block, 0)

    inner = {-1: [3], 0: [0, 1, 2, 3], 1: [0]}
    for d in directions:

        @pl.when(exists(d))
        def _(d=d):
            even, odd = boxes_of(d, 0)
            for i, r in enumerate(inner[d // 3 - 1]):
                for j, c in enumerate(inner[d % 3 - 1]):
                    place = span(d // 3 - 1)[i] * 6 + span(d % 3 - 1)[j]
                    window[place] = (odd if c % 2 else even)[r * 2 + c // 2]

    def forward_row(r, carry):
        for c in range(4):
            a = jnp.zeros((8, 128), F32)
            b = jnp.zeros((8, 128), F32)
            for k in range(2):
                code = codes[r, c, k]
                place = jnp.where(code == 9, 36, (r + code // 3) * 6 + c + code % 3)
                v = window[place].astype(BF16)
                a += nt(v, near[0, r * 4 + c, k])
                b += nt(v, near[1, r * 4 + c, k])
            near_fwd[r * 4 + c] = a + swap(b)
        return carry

    lax.fori_loop(0, 4, forward_row, 0)

    for d in directions:

        @pl.when(exists(d))
        def _(d=d):
            ring_copy(8 - d).wait_recv()
            at = 0
            rows = {-1: [1], 0: [1, 2, 3, 4], 1: [4]}
            for r in rows[d // 3 - 1]:
                for c in rows[d % 3 - 1]:
                    placed[r * 6 + c] += ring_in[d, at]
                    at += 1

    others = gath.at[pl.ds(0, total - 1)]
    pltpu.make_async_copy(others, others, all_recv).wait()

    def coarse_row(rp, carry):
        acc = list(carry)
        ri = row - rp + n_row - 1
        for ci in range(2 * n_col - 1):
            cp = col + n_col - 1 - ci
            there = (cp >= 0) & (cp < n_col)
            apart = (jnp.abs(row - rp) > 1) | (abs(ci - n_col + 1) > 1)
            weight = jnp.where(there & apart, 1.0, 0.0)
            values = gath[rp * n_col + jnp.clip(cp, 0, n_col - 1)].astype(F32)
            for s in range(2):
                rs = ri if s == 0 else 2 * (n_row - 1) - ri
                cs = ci if s == 0 else 2 * (n_col - 1) - ci
                t_re = coarse_tab[0, rs].astype(F32)[cs : cs + 1] * weight
                t_im = coarse_tab[1, rs].astype(F32)[cs : cs + 1] * (weight if s == 0 else -weight)
                v = values[8 * s : 8 * s + 8]
                acc[2 * s] += t_re * v
                acc[2 * s + 1] += t_im * v
        return tuple(acc)

    sums = lax.fori_loop(0, n_row, coarse_row, (jnp.zeros((8, 256), F32),) * 4)

    for s in range(2):
        arrived = sums[2 * s] + swap(sums[2 * s + 1])
        turned = swap(arrived)
        down = [trig[0, j : j + 1] * arrived - trig[1, j : j + 1] * turned for j in range(16)]
        spread = nn(jnp.concatenate(down, 0), interp[...], HIGH)
        incoming = (leaf[s].reshape(128, 128) + spread).astype(BF16)
        both = nn(incoming, w_rcv[s])
        far = both[:, :128].reshape(16, 8, 128) + swap(both[:, 128:].reshape(16, 8, 128))
        out = out_fwd if s == 0 else out_adj
        for j in range(8):
            pair = []
            for b in (2 * j, 2 * j + 1):
                close = near_fwd[b] if s == 0 else placed[(b // 4 + 1) * 6 + b % 4 + 1]
                pair.append(far[b] + close)
            low = upper((8, 128))
            out[0, j] = jnp.where(low, pair[0], pltpu.roll(pair[1], 4, 0))
            out[1, j] = jnp.where(low, pltpu.roll(pair[0], 4, 0), pair[1])

    for d in directions:

        @pl.when(exists(d))
        def _(d=d):
            halo_copy(d).wait_send()
            ring_copy(d).wait_send()

    pltpu.make_async_copy(others, others, all_send).wait()


def per_device(
    n_row,
    n_col,
    current,
    probe,
    near_list,
    near_blocks,
    radiation,
    reception,
    interp,
    phase,
    leaf_table,
    coarse_table,
):
    total = n_row * n_col
    vmem = pl.BlockSpec(memory_space=pltpu.VMEM)
    half = jax.ShapeDtypeStruct((2, 8, 8, 128), F32)
    dma = pltpu.SemaphoreType.DMA
    fwd, adj = pl.pallas_call(
        functools.partial(kernel, n_row, n_col),
        out_shape=(half, half),
        in_specs=[
            vmem,
            vmem,
            pl.BlockSpec(memory_space=pltpu.SMEM),
            pl.BlockSpec(memory_space=pl.ANY),
        ]
        + [vmem] * 6,
        out_specs=(vmem, vmem),
        scratch_shapes=[
            pltpu.VMEM((9, 256, 128), BF16),
            pltpu.VMEM((total, 16, 256), BF16),
            pltpu.VMEM((2, 16, 2, 128, 128), BF16),
            pltpu.VMEM((2, 128, 256), BF16),
            pltpu.VMEM((2, 128, 256), BF16),
            pltpu.VMEM((2, 225, 8, 128), F32),
            pltpu.VMEM((2, 2, 8, 2, 8, 128), F32),
            pltpu.VMEM((2, 16, 8, 128), F32),
            pltpu.VMEM((1, 2, 8, 256), F32),
            pltpu.VMEM((37, 8, 128), F32),
            pltpu.VMEM((36, 8, 128), F32),
            pltpu.VMEM((9, 4, 8, 128), F32),
            pltpu.VMEM((9, 4, 8, 128), F32),
            pltpu.VMEM((16, 8, 128), F32),
            pltpu.VMEM((8, 2, 8, 128), F32),
            pltpu.VMEM((2, 16, 256), F32),
            dma,
            dma((9,)),
            dma((9,)),
            dma((9,)),
            dma((9,)),
            dma,
            dma,
        ],
        compiler_params=pltpu.CompilerParams(
            collective_id=0, has_side_effects=True, vmem_limit_bytes=40 * 1024 * 1024
        ),
        name="operator",
    )(
        current.reshape(128, 128),
        probe.reshape(128, 128),
        near_list,
        near_blocks.reshape(2, 16, 2, 128, 128),
        radiation,
        reception,
        interp,
        phase,
        leaf_table,
        coarse_table,
    )
    return fwd.reshape(current.shape), adj.reshape(current.shape)


def solution(mesh):
    placed = (
        P(None, "row", "col", None, None),
        P(None, "row", "col", None, None),
        P("row", "col", None),
        P(None, "row", "col", None, None, None),
        P(),
        P(),
        P(),
        P(),
        P(),
        P(),
    )
    return jax.shard_map(
        functools.partial(per_device, mesh.shape["row"], mesh.shape["col"]),
        mesh=mesh,
        in_specs=placed,
        out_specs=(P(None, "row", "col", None, None), P(None, "row", "col", None, None)),
        check_vma=False,
    )
```

```python
import functools

import jax
import jax.numpy as jnp
from jax import lax
from jax.experimental import pallas as pl
from jax.experimental.pallas import tpu as pltpu
from jax.sharding import PartitionSpec as P

HIGH = lax.Precision.HIGHEST
F32 = jnp.float32
BF16 = jnp.bfloat16
MESH = pl.DeviceIdType.MESH


def upper(shape):
    return lax.broadcasted_iota(jnp.int32, shape, len(shape) - 2) < 4


def swap(x):
    turned = pltpu.roll(x, 4, x.ndim - 2)
    return jnp.where(upper(x.shape), -turned, turned)


def interleave(re, im):
    low = upper(re.shape)
    return jnp.where(low, re, pltpu.roll(im, 4, 1)), jnp.where(low, pltpu.roll(re, 4, 1), im)


def nn(a, b, precision=None):
    return lax.dot_general(a, b, (((1,), (0,)), ((), ())), precision=precision, preferred_element_type=F32)


def nt(a, b, precision=None):
    return lax.dot_general(a, b, (((1,), (1,)), ((), ())), precision=precision, preferred_element_type=F32)


def kernel(
    n_row,
    n_col,
    cur_hbm,
    prb_hbm,
    codes,
    near_hbm,
    rad_hbm,
    rec_hbm,
    interp_hbm,
    phase_hbm,
    leaf_hbm,
    coarse_hbm,
    out_fwd,
    out_adj,
    rad,
    rec,
    interp,
    phase,
    leaf_tab,
    coarse_tab,
    halo,
    gath,
    near,
    w_rad,
    w_rcv,
    tab,
    patt,
    leaf,
    vec,
    window,
    placed,
    ring_out,
    ring_in,
    near_fwd,
    back,
    trig,
    load_sem,
    halo_send,
    halo_recv,
    ring_send,
    ring_recv,
    all_send,
    all_recv,
):
    row = lax.axis_index("row")
    col = lax.axis_index("col")
    total = n_row * n_col
    me = row * n_col + col

    moves = (
        (cur_hbm, halo.at[4, pl.ds(0, 128)]),
        (prb_hbm, halo.at[4, pl.ds(128, 128)]),
        (rad_hbm, rad),
        (rec_hbm, rec),
        (interp_hbm, interp),
        (phase_hbm, phase),
        (near_hbm, near),
        (leaf_hbm, leaf_tab),
        (coarse_hbm, coarse_tab),
    )
    loads = [pltpu.make_async_copy(src, dst, load_sem.at[i]) for i, (src, dst) in enumerate(moves)]
    for load in loads:
        load.start()
    barrier = pltpu.get_barrier_semaphore()

    def greet(n, carry):
        @pl.when(n != me)
        def _():
            pl.semaphore_signal(barrier, inc=1, device_id=(n // n_col, n % n_col), device_id_type=MESH)

        return carry

    lax.fori_loop(0, total, greet, 0)

    for load in loads[:6]:
        load.wait()
    for x in range(2):
        sign = 1.0 if x == 0 else -1.0
        cols = slice(128 * x, 128 * x + 128)
        rad_f = rad[x].astype(F32)
        rec_f = rec[x].astype(F32)
        w_rad[0, :, cols] = rad_f.T.astype(BF16)
        w_rad[1, :, cols] = (rec_f * sign).astype(BF16)
        w_rcv[0, :, cols] = rec_f.T.astype(BF16)
        w_rcv[1, :, cols] = (rad_f * sign).astype(BF16)
    angles = phase[...]
    trig[0] = jnp.cos(angles)
    trig[1] = jnp.sin(angles)

    def patterns(slot):
        for s in range(2):
            both = nn(halo[slot, 128 * s : 128 * s + 128], w_rad[s])
            re = (both[:64, :128] - both[64:, 128:]).reshape(8, 8, 128)
            im = (both[64:, :128] + both[:64, 128:]).reshape(8, 8, 128)
            even, odd = interleave(re, im)
            patt[s, 0, :, 0] = even
            patt[s, 0, :, 1] = odd
            patt[s, 1, :, 0] = swap(even) if s == 0 else -swap(even)
            patt[s, 1, :, 1] = swap(odd) if s == 0 else -swap(odd)

    def boxes_of(slot, s):
        base = 128 * s
        re = halo[slot, base : base + 64].astype(F32).reshape(8, 8, 128)
        im = halo[slot, base + 64 : base + 128].astype(F32).reshape(8, 8, 128)
        return interleave(re, im)

    patterns(4)
    for s in range(2):
        own = patt[s, 0].reshape(128, 128)
        wide = nt(own, interp[...], HIGH).reshape(16, 8, 256)
        cos_sum = jnp.zeros((8, 256), F32)
        sin_sum = jnp.zeros((8, 256), F32)
        for j in range(16):
            cos_sum += trig[0, j : j + 1] * wide[j]
            sin_sum += trig[1, j : j + 1] * wide[j]
        top = cos_sum + swap(sin_sum)
        vec[0, s] = top
    gath[me] = vec[0].reshape(16, 256).astype(BF16)

    pl.semaphore_wait(barrier, total - 1)

    def halo_copy(d):
        dr = d // 3 - 1
        dc = d % 3 - 1
        return pltpu.make_async_remote_copy(
            src_ref=halo.at[4],
            dst_ref=halo.at[8 - d],
            send_sem=halo_send.at[d],
            recv_sem=halo_recv.at[8 - d],
            device_id=(row + dr, col + dc),
            device_id_type=MESH,
        )

    def exists(d):
        r = row + d // 3 - 1
        c = col + d % 3 - 1
        return (d != 4) & (r >= 0) & (r < n_row) & (c >= 0) & (c < n_col)

    def send_halo(d, carry):
        @pl.when(exists(d))
        def _():
            halo_copy(d).start()

        return carry

    lax.fori_loop(0, 9, send_halo, 0)

    def send_top(n, carry):
        @pl.when(n != me)
        def _():
            pltpu.make_async_remote_copy(
                src_ref=gath.at[me],
                dst_ref=gath.at[me],
                send_sem=all_send,
                recv_sem=all_recv,
                device_id=(n // n_col, n % n_col),
                device_id_type=MESH,
            ).start()

        return carry

    lax.fori_loop(0, total, send_top, 0)

    window[...] = jnp.zeros_like(window)
    placed[...] = jnp.zeros_like(placed)
    even, odd = boxes_of(4, 0)
    for b in range(16):
        window[(b // 4 + 1) * 6 + b % 4 + 1] = (odd if b % 2 else even)[b // 2]
    even, odd = boxes_of(4, 1)
    back[:, 0] = even
    back[:, 1] = odd
    loads[6].wait()

    def adjoint_row(r, carry):
        for c in range(4):
            y = back[r * 2 + c // 2, c % 2].astype(BF16)
            parts = []
            for k in range(2):
                a = nn(y, near[0, r * 4 + c, k])
                b = nn(y, near[1, r * 4 + c, k])
                parts.append(a - swap(b))
            for o in range(9):
                place = (r + o // 3) * 6 + c + o % 3
                term = placed[place]
                for k in range(2):
                    term += jnp.where(codes[r, k, c] == o, 1.0, 0.0) * parts[k]
                placed[place] = term
        return carry

    lax.fori_loop(0, 4, adjoint_row, 0)

    def span(step):
        return {-1: [0], 0: [1, 2, 3, 4], 1: [5]}[step]

    def ring_copy(d):
        dr, dc = d // 3 - 1, d % 3 - 1
        size = 4 if dr == 0 or dc == 0 else 1
        return pltpu.make_async_remote_copy(
            src_ref=ring_out.at[d, pl.ds(0, size)],
            dst_ref=ring_in.at[8 - d, pl.ds(0, size)],
            send_sem=ring_send.at[d],
            recv_sem=ring_recv.at[8 - d],
            device_id=(row + dr, col + dc),
            device_id_type=MESH,
        )

    directions = [d for d in range(9) if d != 4]
    for d in directions:

        @pl.when(exists(d))
        def _(d=d):
            at = 0
            for r in span(d // 3 - 1):
                for c in span(d % 3 - 1):
                    ring_out[d, at] = placed[r * 6 + c]
                    at += 1
            ring_copy(d).start()

    loads[7].wait()

    def spread_table(jr, carry):
        for jc in range(15):
            rows = leaf_tab[jr, jc]
            for x in range(2):
                tab[x, jr * 15 + jc] = jnp.broadcast_to(rows[x : x + 1], (8, 128))
        return carry

    lax.fori_loop(0, 15, spread_table, 0)
    for x in range(2):
        for jr in range(6, 9):
            for jc in range(6, 9):
                tab[x, jr * 15 + jc] = jnp.zeros((8, 128), F32)
    leaf[...] = jnp.zeros_like(leaf)

    def translate(br, bc):
        for s in range(2):

            def source_row(rr, acc, s=s):
                acc = list(acc)
                plain = [patt[s, 0, rr * 2 + cc // 2, cc % 2] for cc in range(4)]
                turned = [patt[s, 1, rr * 2 + cc // 2, cc % 2] for cc in range(4)]
                for r in range(4):
                    for dc in range(-3, 4):
                        at = (br * 4 + rr + 3 - r) * 15 + bc * 4 + dc + 3
                        if s == 1:
                            at = 224 - at
                        t_re = tab[0, at]
                        t_im = tab[1, at]
                        for c in range(4):
                            cc = c + dc
                            if 0 <= cc < 4:
                                acc[r * 4 + c] += t_re * plain[cc] + t_im * turned[cc]
                return tuple(acc)

            acc = lax.fori_loop(0, 4, source_row, tuple(leaf[s, b] for b in range(16)))
            for b in range(16):
                leaf[s, b] = acc[b]

    translate(1, 1)

    def side_block(d, carry):
        @pl.when(exists(d))
        def _():
            halo_copy(8 - d).wait_recv()
            patterns(d)
            translate(d // 3, d % 3)

        return carry

    lax.fori_loop(0, 9, side_block, 0)

    inner = {-1: [3], 0: [0, 1, 2, 3], 1: [0]}
    for d in directions:

        @pl.when(exists(d))
        def _(d=d):
            even, odd = boxes_of(d, 0)
            for i, r in enumerate(inner[d // 3 - 1]):
                for j, c in enumerate(inner[d % 3 - 1]):
                    place = span(d // 3 - 1)[i] * 6 + span(d % 3 - 1)[j]
                    window[place] = (odd if c % 2 else even)[r * 2 + c // 2]

    def forward_row(r, carry):
        for c in range(4):
            a = jnp.zeros((8, 128), F32)
            b = jnp.zeros((8, 128), F32)
            for k in range(2):
                code = codes[r, k, c]
                place = jnp.where(code == 9, 36, (r + code // 3) * 6 + c + code % 3)
                v = window[place].astype(BF16)
                a += nt(v, near[0, r * 4 + c, k])
                b += nt(v, near[1, r * 4 + c, k])
            near_fwd[r * 4 + c] = a + swap(b)
        return carry

    lax.fori_loop(0, 4, forward_row, 0)

    for d in directions:

        @pl.when(exists(d))
        def _(d=d):
            ring_copy(8 - d).wait_recv()
            at = 0
            rows = {-1: [1], 0: [1, 2, 3, 4], 1: [4]}
            for r in rows[d // 3 - 1]:
                for c in rows[d % 3 - 1]:
                    placed[r * 6 + c] += ring_in[d, at]
                    at += 1

    others = gath.at[pl.ds(0, total - 1)]
    pltpu.make_async_copy(others, others, all_recv).wait()

    loads[8].wait()

    def coarse_row(rp, carry):
        acc = list(carry)
        ri = row - rp + n_row - 1
        for cp in range(n_col):
            ci = col - cp + n_col - 1
            apart = (jnp.abs(row - rp) > 1) | (jnp.abs(col - cp) > 1)
            weight = jnp.where(apart, 1.0, 0.0)
            values = gath[rp * n_col + cp].astype(F32)
            for s in range(2):
                rs = ri if s == 0 else 2 * (n_row - 1) - ri
                cs = ci if s == 0 else 2 * (n_col - 1) - ci
                coeff = coarse_tab[rs, cs].astype(F32)
                t_re = coeff[0:1] * weight
                t_im = coeff[1:2] * (weight if s == 0 else -weight)
                v = values[8 * s : 8 * s + 8]
                acc[2 * s] += t_re * v
                acc[2 * s + 1] += t_im * v
        return tuple(acc)

    sums = lax.fori_loop(0, n_row, coarse_row, (jnp.zeros((8, 256), F32),) * 4)

    for s in range(2):
        arrived = sums[2 * s] + swap(sums[2 * s + 1])
        turned = swap(arrived)
        down = [trig[0, j : j + 1] * arrived - trig[1, j : j + 1] * turned for j in range(16)]
        spread = nn(jnp.concatenate(down, 0), interp[...], HIGH)
        incoming = (leaf[s].reshape(128, 128) + spread).astype(BF16)
        both = nn(incoming, w_rcv[s])
        far = both[:, :128].reshape(16, 8, 128) + swap(both[:, 128:].reshape(16, 8, 128))
        out = out_fwd if s == 0 else out_adj
        for j in range(8):
            pair = []
            for b in (2 * j, 2 * j + 1):
                close = near_fwd[b] if s == 0 else placed[(b // 4 + 1) * 6 + b % 4 + 1]
                pair.append(far[b] + close)
            low = upper((8, 128))
            out[0, j] = jnp.where(low, pair[0], pltpu.roll(pair[1], 4, 0))
            out[1, j] = jnp.where(low, pltpu.roll(pair[0], 4, 0), pair[1])

    for d in directions:

        @pl.when(exists(d))
        def _(d=d):
            halo_copy(d).wait_send()
            ring_copy(d).wait_send()

    pltpu.make_async_copy(others, others, all_send).wait()


def per_device(
    n_row,
    n_col,
    current,
    probe,
    near_list,
    near_blocks,
    radiation,
    reception,
    interp,
    phase,
    leaf_table,
    coarse_table,
):
    total = n_row * n_col
    vmem = pl.BlockSpec(memory_space=pltpu.VMEM)
    hbm = pl.BlockSpec(memory_space=pltpu.HBM)
    leaf_rows = jnp.transpose(leaf_table, (1, 2, 0, 3))
    coarse_rows = jnp.transpose(coarse_table, (1, 2, 0, 3))
    half = jax.ShapeDtypeStruct((2, 8, 8, 128), F32)
    dma = pltpu.SemaphoreType.DMA
    fwd, adj = pl.pallas_call(
        functools.partial(kernel, n_row, n_col),
        out_shape=(half, half),
        in_specs=[hbm, hbm, pl.BlockSpec(memory_space=pltpu.SMEM)] + [hbm] * 7,
        out_specs=(vmem, vmem),
        scratch_shapes=[
            pltpu.VMEM(radiation.shape, BF16),
            pltpu.VMEM(reception.shape, BF16),
            pltpu.VMEM(interp.shape, F32),
            pltpu.VMEM(phase.shape, F32),
            pltpu.VMEM(leaf_rows.shape, F32),
            pltpu.VMEM(coarse_rows.shape, BF16),
            pltpu.VMEM((9, 256, 128), BF16),
            pltpu.VMEM((total, 16, 256), BF16),
            pltpu.VMEM((2, 16, 2, 128, 128), BF16),
            pltpu.VMEM((2, 128, 256), BF16),
            pltpu.VMEM((2, 128, 256), BF16),
            pltpu.VMEM((2, 225, 8, 128), F32),
            pltpu.VMEM((2, 2, 8, 2, 8, 128), F32),
            pltpu.VMEM((2, 16, 8, 128), F32),
            pltpu.VMEM((1, 2, 8, 256), F32),
            pltpu.VMEM((37, 8, 128), F32),
            pltpu.VMEM((36, 8, 128), F32),
            pltpu.VMEM((9, 4, 8, 128), F32),
            pltpu.VMEM((9, 4, 8, 128), F32),
            pltpu.VMEM((16, 8, 128), F32),
            pltpu.VMEM((8, 2, 8, 128), F32),
            pltpu.VMEM((2, 16, 256), F32),
            dma((9,)),
            dma((9,)),
            dma((9,)),
            dma((9,)),
            dma((9,)),
            dma,
            dma,
        ],
        compiler_params=pltpu.CompilerParams(
            collective_id=0, has_side_effects=True, vmem_limit_bytes=63 * 1024 * 1024
        ),
        name="operator",
    )(
        current.reshape(128, 128),
        probe.reshape(128, 128),
        jnp.transpose(near_list, (0, 2, 1)),
        near_blocks.reshape(2, 16, 2, 128, 128),
        radiation,
        reception,
        interp,
        phase,
        leaf_rows,
        coarse_rows,
    )
    return fwd.reshape(current.shape), adj.reshape(current.shape)


def solution(mesh):
    placed = (
        P(None, "row", "col", None, None),
        P(None, "row", "col", None, None),
        P("row", "col", None),
        P(None, "row", "col", None, None, None),
        P(),
        P(),
        P(),
        P(),
        P(),
        P(),
    )
    return jax.shard_map(
        functools.partial(per_device, mesh.shape["row"], mesh.shape["col"]),
        mesh=mesh,
        in_specs=placed,
        out_specs=(P(None, "row", "col", None, None), P(None, "row", "col", None, None)),
        check_vma=False,
    )
```

```python
import functools

import jax
import jax.numpy as jnp
from jax import lax
from jax.experimental import pallas as pl
from jax.experimental.pallas import tpu as pltpu
from jax.sharding import PartitionSpec as P

HIGH = lax.Precision.HIGHEST
F32 = jnp.float32
BF16 = jnp.bfloat16
MESH = pl.DeviceIdType.MESH


def upper(shape):
    return lax.broadcasted_iota(jnp.int32, shape, len(shape) - 2) < 4


def swap(x):
    turned = pltpu.roll(x, 4, x.ndim - 2)
    return jnp.where(upper(x.shape), -turned, turned)


def interleave(re, im):
    low = upper(re.shape)
    return jnp.where(low, re, pltpu.roll(im, 4, 1)), jnp.where(low, pltpu.roll(re, 4, 1), im)


def nn(a, b, precision=None):
    return lax.dot_general(a, b, (((1,), (0,)), ((), ())), precision=precision, preferred_element_type=F32)


def nt(a, b, precision=None):
    return lax.dot_general(a, b, (((1,), (1,)), ((), ())), precision=precision, preferred_element_type=F32)


def kernel(
    n_row,
    n_col,
    cur_hbm,
    prb_hbm,
    codes,
    near_hbm,
    rad_hbm,
    rec_hbm,
    interp_hbm,
    phase_hbm,
    leaf_hbm,
    coarse_hbm,
    out_fwd,
    out_adj,
    rad,
    rec,
    interp,
    phase,
    leaf_tab,
    coarse_tab,
    halo,
    gath,
    near,
    w_rad,
    w_rcv,
    tab,
    patt,
    leaf,
    vec,
    window,
    placed,
    ring_out,
    ring_in,
    near_fwd,
    back,
    trig,
    load_sem,
    halo_send,
    halo_recv,
    ring_send,
    ring_recv,
    all_send,
    all_recv,
):
    row = lax.axis_index("row")
    col = lax.axis_index("col")

    moves = (
        (cur_hbm, halo.at[4, pl.ds(0, 128)]),
        (prb_hbm, halo.at[4, pl.ds(128, 128)]),
        (rad_hbm, rad),
        (rec_hbm, rec),
        (interp_hbm, interp),
        (phase_hbm, phase),
        (near_hbm, near),
        (leaf_hbm, leaf_tab),
        (coarse_hbm, coarse_tab),
    )
    loads = [pltpu.make_async_copy(src, dst, load_sem.at[i]) for i, (src, dst) in enumerate(moves)]
    for load in loads:
        load.start()
    barrier = pltpu.get_barrier_semaphore()

    def exists(d):
        r = row + d // 3 - 1
        c = col + d % 3 - 1
        return (d != 4) & (r >= 0) & (r < n_row) & (c >= 0) & (c < n_col)

    def greet(r, c):
        pl.semaphore_signal(barrier, inc=1, device_id=(r, c), device_id_type=MESH)

    def greet_rows(n, carry):
        @pl.when(n != row)
        def _():
            greet(n, col)

        return carry

    def greet_cols(n, carry):
        @pl.when(n != col)
        def _():
            greet(row, n)

        return carry

    lax.fori_loop(0, n_row, greet_rows, 0)
    lax.fori_loop(0, n_col, greet_cols, 0)
    peers = n_row + n_col - 2
    for d in (0, 2, 6, 8):
        peers += jnp.where(exists(d), 1, 0)

        @pl.when(exists(d))
        def _(d=d):
            greet(row + d // 3 - 1, col + d % 3 - 1)

    pl.semaphore_wait(barrier, peers)

    def halo_copies(d, to, slot, first):
        sources = (cur_hbm, prb_hbm) if first else tuple(halo.at[d, pl.ds(128 * i, 128)] for i in range(2))
        return [
            pltpu.make_async_remote_copy(
                src_ref=sources[i],
                dst_ref=halo.at[slot, pl.ds(128 * i, 128)],
                send_sem=halo_send.at[i, d + to - 4],
                recv_sem=halo_recv.at[i, slot],
                device_id=(row + to // 3 - 1, col + to % 3 - 1),
                device_id_type=MESH,
            )
            for i in range(2)
        ]

    for d in (1, 7, 3, 5):

        @pl.when(exists(d))
        def _(d=d):
            for copy in halo_copies(4, d, 8 - d, True):
                copy.start()

    for load in loads[:6]:
        load.wait()
    for x in range(2):
        sign = 1.0 if x == 0 else -1.0
        cols = slice(128 * x, 128 * x + 128)
        rad_f = rad[x].astype(F32)
        rec_f = rec[x].astype(F32)
        w_rad[0, :, cols] = rad_f.T.astype(BF16)
        w_rad[1, :, cols] = (rec_f * sign).astype(BF16)
        w_rcv[0, :, cols] = rec_f.T.astype(BF16)
        w_rcv[1, :, cols] = (rad_f * sign).astype(BF16)
    angles = phase[...]
    trig[0] = jnp.cos(angles)
    trig[1] = jnp.sin(angles)

    def patterns(slot):
        for s in range(2):
            both = nn(halo[slot, 128 * s : 128 * s + 128], w_rad[s])
            re = (both[:64, :128] - both[64:, 128:]).reshape(8, 8, 128)
            im = (both[64:, :128] + both[:64, 128:]).reshape(8, 8, 128)
            even, odd = interleave(re, im)
            patt[s, 0, :, 0] = even
            patt[s, 0, :, 1] = odd
            patt[s, 1, :, 0] = swap(even) if s == 0 else -swap(even)
            patt[s, 1, :, 1] = swap(odd) if s == 0 else -swap(odd)

    def boxes_of(slot, s):
        base = 128 * s
        re = halo[slot, base : base + 64].astype(F32).reshape(8, 8, 128)
        im = halo[slot, base + 64 : base + 128].astype(F32).reshape(8, 8, 128)
        return interleave(re, im)

    patterns(4)
    for s in range(2):
        own = patt[s, 0].reshape(128, 128)
        wide = nt(own, interp[...], HIGH).reshape(16, 8, 256)
        cos_sum = jnp.zeros((8, 256), F32)
        sin_sum = jnp.zeros((8, 256), F32)
        for j in range(16):
            cos_sum += trig[0, j : j + 1] * wide[j]
            sin_sum += trig[1, j : j + 1] * wide[j]
        top = cos_sum + swap(sin_sum)
        vec[0, s] = top
    gath[col, row] = vec[0].reshape(16, 256).astype(BF16)

    def top_copy(r):
        return pltpu.make_async_remote_copy(
            src_ref=gath.at[col, row],
            dst_ref=gath.at[col, row],
            send_sem=all_send.at[0],
            recv_sem=all_recv.at[0],
            device_id=(r, col),
            device_id_type=MESH,
        )

    def send_top(n, carry):
        @pl.when(n != row)
        def _():
            top_copy(n).start()

        return carry

    lax.fori_loop(0, n_row, send_top, 0)

    window[...] = jnp.zeros_like(window)
    placed[...] = jnp.zeros_like(placed)
    even, odd = boxes_of(4, 0)
    for b in range(16):
        window[(b // 4 + 1) * 6 + b % 4 + 1] = (odd if b % 2 else even)[b // 2]
    even, odd = boxes_of(4, 1)
    back[:, 0] = even
    back[:, 1] = odd
    loads[6].wait()

    def adjoint_row(r, carry):
        for c in range(4):
            y = back[r * 2 + c // 2, c % 2].astype(BF16)
            parts = []
            for k in range(2):
                a = nn(y, near[0, r * 4 + c, k])
                b = nn(y, near[1, r * 4 + c, k])
                parts.append(a - swap(b))
            for o in range(9):
                place = (r + o // 3) * 6 + c + o % 3
                term = placed[place]
                for k in range(2):
                    term += jnp.where(codes[r, k, c] == o, 1.0, 0.0) * parts[k]
                placed[place] = term
        return carry

    lax.fori_loop(0, 4, adjoint_row, 0)

    def span(step):
        return {-1: [0], 0: [1, 2, 3, 4], 1: [5]}[step]

    def ring_copy(d):
        dr, dc = d // 3 - 1, d % 3 - 1
        size = 4 if dr == 0 or dc == 0 else 1
        return pltpu.make_async_remote_copy(
            src_ref=ring_out.at[d, pl.ds(0, size)],
            dst_ref=ring_in.at[8 - d, pl.ds(0, size)],
            send_sem=ring_send.at[d],
            recv_sem=ring_recv.at[8 - d],
            device_id=(row + dr, col + dc),
            device_id_type=MESH,
        )

    directions = [d for d in range(9) if d != 4]
    for d in directions:

        @pl.when(exists(d))
        def _(d=d):
            at = 0
            for r in span(d // 3 - 1):
                for c in span(d % 3 - 1):
                    ring_out[d, at] = placed[r * 6 + c]
                    at += 1
            ring_copy(d).start()

    for d in (1, 7):

        @pl.when(exists(d))
        def _(d=d):
            for copy in halo_copies(4, d, d, False):
                copy.wait_recv()
            for to in (3, 5):

                @pl.when(exists(to))
                def _(to=to):
                    for copy in halo_copies(d, to, d + 4 - to, False):
                        copy.start()

    loads[7].wait()

    def spread_table(jr, carry):
        for jc in range(15):
            rows = leaf_tab[jr, jc]
            for x in range(2):
                tab[x, jr * 15 + jc] = jnp.broadcast_to(rows[x : x + 1], (8, 128))
        return carry

    lax.fori_loop(0, 15, spread_table, 0)
    for x in range(2):
        for jr in range(6, 9):
            for jc in range(6, 9):
                tab[x, jr * 15 + jc] = jnp.zeros((8, 128), F32)
    leaf[...] = jnp.zeros_like(leaf)

    def translate(br, bc):
        for s in range(2):

            def source_row(rr, acc, s=s):
                acc = list(acc)
                plain = [patt[s, 0, rr * 2 + cc // 2, cc % 2] for cc in range(4)]
                turned = [patt[s, 1, rr * 2 + cc // 2, cc % 2] for cc in range(4)]
                for r in range(4):
                    for dc in range(-3, 4):
                        at = (br * 4 + rr + 3 - r) * 15 + bc * 4 + dc + 3
                        if s == 1:
                            at = 224 - at
                        t_re = tab[0, at]
                        t_im = tab[1, at]
                        for c in range(4):
                            cc = c + dc
                            if 0 <= cc < 4:
                                acc[r * 4 + c] += t_re * plain[cc] + t_im * turned[cc]
                return tuple(acc)

            acc = lax.fori_loop(0, 4, source_row, tuple(leaf[s, b] for b in range(16)))
            for b in range(16):
                leaf[s, b] = acc[b]

    translate(1, 1)

    column = gath.at[0, pl.ds(0, n_row - 1)]
    pltpu.make_async_copy(column, column, all_recv.at[0]).wait()

    def send_column(n, carry):
        @pl.when(n != col)
        def _():
            pltpu.make_async_remote_copy(
                src_ref=gath.at[col],
                dst_ref=gath.at[col],
                send_sem=all_send.at[1],
                recv_sem=all_recv.at[1],
                device_id=(row, n),
                device_id_type=MESH,
            ).start()

        return carry

    lax.fori_loop(0, n_col, send_column, 0)

    def side_block(d):
        patterns(d)
        translate(d // 3, d % 3)

    def direct_block(i, carry):
        d = 1 + 6 * i

        @pl.when(exists(d))
        def _():
            side_block(d)

        return carry

    lax.fori_loop(0, 2, direct_block, 0)

    def across_block(i, carry):
        d = (i // 2 + 1) % 3 * 3 + i % 2 * 2

        @pl.when(exists(d))
        def _():
            for copy in halo_copies(4, d, d, False):
                copy.wait_recv()
            side_block(d)

        return carry

    lax.fori_loop(0, 6, across_block, 0)

    inner = {-1: [3], 0: [0, 1, 2, 3], 1: [0]}
    for d in directions:

        @pl.when(exists(d))
        def _(d=d):
            even, odd = boxes_of(d, 0)
            for i, r in enumerate(inner[d // 3 - 1]):
                for j, c in enumerate(inner[d % 3 - 1]):
                    place = span(d // 3 - 1)[i] * 6 + span(d % 3 - 1)[j]
                    window[place] = (odd if c % 2 else even)[r * 2 + c // 2]

    def forward_row(r, carry):
        for c in range(4):
            a = jnp.zeros((8, 128), F32)
            b = jnp.zeros((8, 128), F32)
            for k in range(2):
                code = codes[r, k, c]
                place = jnp.where(code == 9, 36, (r + code // 3) * 6 + c + code % 3)
                v = window[place].astype(BF16)
                a += nt(v, near[0, r * 4 + c, k])
                b += nt(v, near[1, r * 4 + c, k])
            near_fwd[r * 4 + c] = a + swap(b)
        return carry

    lax.fori_loop(0, 4, forward_row, 0)

    for d in directions:

        @pl.when(exists(d))
        def _(d=d):
            ring_copy(8 - d).wait_recv()
            at = 0
            rows = {-1: [1], 0: [1, 2, 3, 4], 1: [4]}
            for r in rows[d // 3 - 1]:
                for c in rows[d % 3 - 1]:
                    placed[r * 6 + c] += ring_in[d, at]
                    at += 1

    others = gath.at[pl.ds(0, n_col - 1)]
    pltpu.make_async_copy(others, others, all_recv.at[1]).wait()
    loads[8].wait()

    def coarse_row(rp, carry):
        acc = list(carry)
        ri = row - rp + n_row - 1
        for cp in range(n_col):
            ci = col - cp + n_col - 1
            apart = (jnp.abs(row - rp) > 1) | (jnp.abs(col - cp) > 1)
            weight = jnp.where(apart, 1.0, 0.0)
            values = gath[cp, rp].astype(F32)
            for s in range(2):
                rs = ri if s == 0 else 2 * (n_row - 1) - ri
                cs = ci if s == 0 else 2 * (n_col - 1) - ci
                coeff = coarse_tab[rs, cs].astype(F32)
                t_re = coeff[0:1] * weight
                t_im = coeff[1:2] * (weight if s == 0 else -weight)
                v = values[8 * s : 8 * s + 8]
                acc[2 * s] += t_re * v
                acc[2 * s + 1] += t_im * v
        return tuple(acc)

    sums = lax.fori_loop(0, n_row, coarse_row, (jnp.zeros((8, 256), F32),) * 4)

    for s in range(2):
        arrived = sums[2 * s] + swap(sums[2 * s + 1])
        turned = swap(arrived)
        down = [trig[0, j : j + 1] * arrived - trig[1, j : j + 1] * turned for j in range(16)]
        spread = nn(jnp.concatenate(down, 0), interp[...], HIGH)
        incoming = (leaf[s].reshape(128, 128) + spread).astype(BF16)
        both = nn(incoming, w_rcv[s])
        far = both[:, :128].reshape(16, 8, 128) + swap(both[:, 128:].reshape(16, 8, 128))
        out = out_fwd if s == 0 else out_adj
        for j in range(8):
            pair = []
            for b in (2 * j, 2 * j + 1):
                close = near_fwd[b] if s == 0 else placed[(b // 4 + 1) * 6 + b % 4 + 1]
                pair.append(far[b] + close)
            low = upper((8, 128))
            out[0, j] = jnp.where(low, pair[0], pltpu.roll(pair[1], 4, 0))
            out[1, j] = jnp.where(low, pltpu.roll(pair[0], 4, 0), pair[1])

    for d in directions:

        @pl.when(exists(d))
        def _(d=d):
            for copy in halo_copies(4, d, 8 - d, d % 2 == 1):
                copy.wait_send()
            ring_copy(d).wait_send()

    pltpu.make_async_copy(column, column, all_send.at[0]).wait()
    pltpu.make_async_copy(others, others, all_send.at[1]).wait()


def per_device(
    n_row,
    n_col,
    current,
    probe,
    near_list,
    near_blocks,
    radiation,
    reception,
    interp,
    phase,
    leaf_table,
    coarse_table,
):
    vmem = pl.BlockSpec(memory_space=pltpu.VMEM)
    hbm = pl.BlockSpec(memory_space=pltpu.HBM)
    leaf_rows = jnp.transpose(leaf_table, (1, 2, 0, 3))
    coarse_rows = jnp.transpose(coarse_table, (1, 2, 0, 3))
    half = pltpu.VMEM((2, 8, 8, 128), F32)
    dma = pltpu.SemaphoreType.DMA
    fwd, adj = pl.pallas_call(
        functools.partial(kernel, n_row, n_col),
        out_shape=(half, half),
        in_specs=[hbm, hbm, pl.BlockSpec(memory_space=pltpu.SMEM)] + [hbm] * 7,
        out_specs=(vmem, vmem),
        scratch_shapes=[
            pltpu.VMEM(radiation.shape, BF16),
            pltpu.VMEM(reception.shape, BF16),
            pltpu.VMEM(interp.shape, F32),
            pltpu.VMEM(phase.shape, F32),
            pltpu.VMEM(leaf_rows.shape, F32),
            pltpu.VMEM(coarse_rows.shape, BF16),
            pltpu.VMEM((9, 256, 128), BF16),
            pltpu.VMEM((n_col, n_row, 16, 256), BF16),
            pltpu.VMEM((2, 16, 2, 128, 128), BF16),
            pltpu.VMEM((2, 128, 256), BF16),
            pltpu.VMEM((2, 128, 256), BF16),
            pltpu.VMEM((2, 225, 8, 128), F32),
            pltpu.VMEM((2, 2, 8, 2, 8, 128), F32),
            pltpu.VMEM((2, 16, 8, 128), F32),
            pltpu.VMEM((1, 2, 8, 256), F32),
            pltpu.VMEM((37, 8, 128), F32),
            pltpu.VMEM((36, 8, 128), F32),
            pltpu.VMEM((9, 4, 8, 128), F32),
            pltpu.VMEM((9, 4, 8, 128), F32),
            pltpu.VMEM((16, 8, 128), F32),
            pltpu.VMEM((8, 2, 8, 128), F32),
            pltpu.VMEM((2, 16, 256), F32),
            dma((9,)),
            dma((2, 9)),
            dma((2, 9)),
            dma((9,)),
            dma((9,)),
            dma((2,)),
            dma((2,)),
        ],
        compiler_params=pltpu.CompilerParams(
            collective_id=0, has_side_effects=True, vmem_limit_bytes=63 * 1024 * 1024
        ),
        name="operator",
    )(
        current.reshape(128, 128),
        probe.reshape(128, 128),
        jnp.transpose(near_list, (0, 2, 1)),
        near_blocks.reshape(2, 16, 2, 128, 128),
        radiation,
        reception,
        interp,
        phase,
        leaf_rows,
        coarse_rows,
    )
    return fwd.reshape(current.shape), adj.reshape(current.shape)


def solution(mesh):
    placed = (
        P(None, "row", "col", None, None),
        P(None, "row", "col", None, None),
        P("row", "col", None),
        P(None, "row", "col", None, None, None),
        P(),
        P(),
        P(),
        P(),
        P(),
        P(),
    )
    return jax.shard_map(
        functools.partial(per_device, mesh.shape["row"], mesh.shape["col"]),
        mesh=mesh,
        in_specs=placed,
        out_specs=(P(None, "row", "col", None, None), P(None, "row", "col", None, None)),
        check_vma=False,
    )
```

```python
import functools

import jax
import jax.numpy as jnp
from jax import lax
from jax.experimental import pallas as pl
from jax.experimental.pallas import tpu as pltpu
from jax.sharding import PartitionSpec as P

HIGH = lax.Precision.HIGHEST
F32 = jnp.float32
BF16 = jnp.bfloat16
MESH = pl.DeviceIdType.MESH


def upper(shape):
    return lax.broadcasted_iota(jnp.int32, shape, len(shape) - 2) < 4


def swap(x):
    turned = pltpu.roll(x, 4, x.ndim - 2)
    return jnp.where(upper(x.shape), -turned, turned)


def interleave(re, im):
    low = upper(re.shape)
    return jnp.where(low, re, pltpu.roll(im, 4, 1)), jnp.where(low, pltpu.roll(re, 4, 1), im)


def nn(a, b, precision=None):
    return lax.dot_general(a, b, (((1,), (0,)), ((), ())), precision=precision, preferred_element_type=F32)


def nt(a, b, precision=None):
    return lax.dot_general(a, b, (((1,), (1,)), ((), ())), precision=precision, preferred_element_type=F32)


def kernel(
    n_row,
    n_col,
    cur_hbm,
    prb_hbm,
    codes,
    near_hbm,
    rad_hbm,
    rec_hbm,
    interp_hbm,
    phase_hbm,
    leaf_hbm,
    coarse_hbm,
    out_fwd,
    out_adj,
    rad,
    rec,
    interp,
    phase,
    leaf_tab,
    coarse_tab,
    halo,
    gath,
    near,
    w_rad,
    w_rcv,
    tab,
    patt,
    leaf,
    vec,
    window,
    placed,
    ring_out,
    ring_in,
    near_fwd,
    back,
    trig,
    load_sem,
    halo_send,
    halo_recv,
    ring_send,
    ring_recv,
    all_send,
    all_recv,
):
    row = lax.axis_index("row")
    col = lax.axis_index("col")

    moves = (
        (cur_hbm, halo.at[4, pl.ds(0, 128)]),
        (prb_hbm, halo.at[4, pl.ds(128, 128)]),
        (rad_hbm, rad),
        (rec_hbm, rec),
        (interp_hbm, interp),
        (phase_hbm, phase),
        (near_hbm, near),
        (leaf_hbm, leaf_tab),
        (coarse_hbm, coarse_tab),
    )
    loads = [pltpu.make_async_copy(src, dst, load_sem.at[i]) for i, (src, dst) in enumerate(moves)]
    barrier = pltpu.get_barrier_semaphore()

    def exists(d):
        r = row + d // 3 - 1
        c = col + d % 3 - 1
        return (d != 4) & (r >= 0) & (r < n_row) & (c >= 0) & (c < n_col)

    def greet(r, c):
        pl.semaphore_signal(barrier, inc=1, device_id=(r, c), device_id_type=MESH)

    def greet_rows(n, carry):
        @pl.when(n != row)
        def _():
            greet(n, col)

        return carry

    def greet_cols(n, carry):
        @pl.when(n != col)
        def _():
            greet(row, n)

        return carry

    lax.fori_loop(0, n_row, greet_rows, 0)
    lax.fori_loop(0, n_col, greet_cols, 0)
    peers = n_row + n_col - 2
    for d in (0, 2, 6, 8):
        peers += jnp.where(exists(d), 1, 0)

        @pl.when(exists(d))
        def _(d=d):
            greet(row + d // 3 - 1, col + d % 3 - 1)

    for load in loads:
        load.start()
    pl.semaphore_wait(barrier, peers)

    def halo_copies(d, to, slot, first):
        sources = (cur_hbm, prb_hbm) if first else tuple(halo.at[d, pl.ds(128 * i, 128)] for i in range(2))
        return [
            pltpu.make_async_remote_copy(
                src_ref=sources[i],
                dst_ref=halo.at[slot, pl.ds(128 * i, 128)],
                send_sem=halo_send.at[i, d + to - 4],
                recv_sem=halo_recv.at[i, slot],
                device_id=(row + to // 3 - 1, col + to % 3 - 1),
                device_id_type=MESH,
            )
            for i in range(2)
        ]

    for d in (1, 7, 3, 5):

        @pl.when(exists(d))
        def _(d=d):
            for copy in halo_copies(4, d, 8 - d, True):
                copy.start()

    for load in loads[:6]:
        load.wait()
    for x in range(2):
        sign = 1.0 if x == 0 else -1.0
        cols = slice(128 * x, 128 * x + 128)
        rad_f = rad[x].astype(F32)
        rec_f = rec[x].astype(F32)
        w_rad[0, :, cols] = rad_f.T.astype(BF16)
        w_rad[1, :, cols] = (rec_f * sign).astype(BF16)
        w_rcv[0, :, cols] = rec_f.T.astype(BF16)
        w_rcv[1, :, cols] = (rad_f * sign).astype(BF16)
    angles = phase[...]
    trig[0] = jnp.cos(angles)
    trig[1] = jnp.sin(angles)

    def patterns(slot):
        for s in range(2):
            both = nn(halo[slot, 128 * s : 128 * s + 128], w_rad[s])
            re = (both[:64, :128] - both[64:, 128:]).reshape(8, 8, 128)
            im = (both[64:, :128] + both[:64, 128:]).reshape(8, 8, 128)
            even, odd = interleave(re, im)
            patt[s, 0, :, 0] = even
            patt[s, 0, :, 1] = odd
            patt[s, 1, :, 0] = swap(even) if s == 0 else -swap(even)
            patt[s, 1, :, 1] = swap(odd) if s == 0 else -swap(odd)

    def boxes_of(slot, s):
        base = 128 * s
        re = halo[slot, base : base + 64].astype(F32).reshape(8, 8, 128)
        im = halo[slot, base + 64 : base + 128].astype(F32).reshape(8, 8, 128)
        return interleave(re, im)

    patterns(4)
    for s in range(2):
        own = patt[s, 0].reshape(128, 128)
        wide = nt(own, interp[...], HIGH).reshape(16, 8, 256)
        cos_sum = jnp.zeros((8, 256), F32)
        sin_sum = jnp.zeros((8, 256), F32)
        for j in range(16):
            cos_sum += trig[0, j : j + 1] * wide[j]
            sin_sum += trig[1, j : j + 1] * wide[j]
        top = cos_sum + swap(sin_sum)
        vec[0, s] = top
    gath[col, row] = vec[0].reshape(16, 256).astype(BF16)

    def top_copy(r):
        return pltpu.make_async_remote_copy(
            src_ref=gath.at[col, row],
            dst_ref=gath.at[col, row],
            send_sem=all_send.at[0],
            recv_sem=all_recv.at[0],
            device_id=(r, col),
            device_id_type=MESH,
        )

    def send_top(n, carry):
        @pl.when(n != row)
        def _():
            top_copy(n).start()

        return carry

    lax.fori_loop(0, n_row, send_top, 0)

    window[...] = jnp.zeros_like(window)
    placed[...] = jnp.zeros_like(placed)
    even, odd = boxes_of(4, 0)
    for b in range(16):
        window[(b // 4 + 1) * 6 + b % 4 + 1] = (odd if b % 2 else even)[b // 2]
    even, odd = boxes_of(4, 1)
    back[:, 0] = even
    back[:, 1] = odd
    loads[6].wait()

    def adjoint_row(r, carry):
        for c in range(4):
            y = back[r * 2 + c // 2, c % 2].astype(BF16)
            parts = []
            for k in range(2):
                a = nn(y, near[0, r * 4 + c, k])
                b = nn(y, near[1, r * 4 + c, k])
                parts.append(a - swap(b))
            for o in range(9):
                place = (r + o // 3) * 6 + c + o % 3
                term = placed[place]
                for k in range(2):
                    term += jnp.where(codes[r, k, c] == o, 1.0, 0.0) * parts[k]
                placed[place] = term
        return carry

    lax.fori_loop(0, 4, adjoint_row, 0)

    def span(step):
        return {-1: [0], 0: [1, 2, 3, 4], 1: [5]}[step]

    def ring_copy(d):
        dr, dc = d // 3 - 1, d % 3 - 1
        size = 4 if dr == 0 or dc == 0 else 1
        return pltpu.make_async_remote_copy(
            src_ref=ring_out.at[d, pl.ds(0, size)],
            dst_ref=ring_in.at[8 - d, pl.ds(0, size)],
            send_sem=ring_send.at[d],
            recv_sem=ring_recv.at[8 - d],
            device_id=(row + dr, col + dc),
            device_id_type=MESH,
        )

    directions = [d for d in range(9) if d != 4]
    for d in directions:

        @pl.when(exists(d))
        def _(d=d):
            at = 0
            for r in span(d // 3 - 1):
                for c in span(d % 3 - 1):
                    ring_out[d, at] = placed[r * 6 + c]
                    at += 1
            ring_copy(d).start()

    for d in (1, 7):

        @pl.when(exists(d))
        def _(d=d):
            for copy in halo_copies(4, d, d, False):
                copy.wait_recv()
            for to in (3, 5):

                @pl.when(exists(to))
                def _(to=to):
                    for copy in halo_copies(d, to, d + 4 - to, False):
                        copy.start()

    loads[7].wait()

    def spread_table(jr, carry):
        for jc in range(15):
            rows = leaf_tab[jr, jc]
            for x in range(2):
                tab[x, jr * 15 + jc] = jnp.broadcast_to(rows[x : x + 1], (8, 128))
        return carry

    lax.fori_loop(0, 15, spread_table, 0)
    for x in range(2):
        for jr in range(6, 9):
            for jc in range(6, 9):
                tab[x, jr * 15 + jc] = jnp.zeros((8, 128), F32)
    leaf[...] = jnp.zeros_like(leaf)

    def translate(br, bc):
        for s in range(2):

            def source_row(rr, acc, s=s):
                acc = list(acc)
                plain = [patt[s, 0, rr * 2 + cc // 2, cc % 2] for cc in range(4)]
                turned = [patt[s, 1, rr * 2 + cc // 2, cc % 2] for cc in range(4)]
                for r in range(4):
                    for dc in range(-3, 4):
                        at = (br * 4 + rr + 3 - r) * 15 + bc * 4 + dc + 3
                        if s == 1:
                            at = 224 - at
                        t_re = tab[0, at]
                        t_im = tab[1, at]
                        for c in range(4):
                            cc = c + dc
                            if 0 <= cc < 4:
                                acc[r * 4 + c] += t_re * plain[cc] + t_im * turned[cc]
                return tuple(acc)

            acc = lax.fori_loop(0, 4, source_row, tuple(leaf[s, b] for b in range(16)))
            for b in range(16):
                leaf[s, b] = acc[b]

    translate(1, 1)

    column = gath.at[0, pl.ds(0, n_row - 1)]
    pltpu.make_async_copy(column, column, all_recv.at[0]).wait()

    def send_column(n, carry):
        @pl.when(n != col)
        def _():
            pltpu.make_async_remote_copy(
                src_ref=gath.at[col],
                dst_ref=gath.at[col],
                send_sem=all_send.at[1],
                recv_sem=all_recv.at[1],
                device_id=(row, n),
                device_id_type=MESH,
            ).start()

        return carry

    lax.fori_loop(0, n_col, send_column, 0)

    def side_block(d):
        patterns(d)
        translate(d // 3, d % 3)

    def direct_block(i, carry):
        d = 1 + 6 * i

        @pl.when(exists(d))
        def _():
            side_block(d)

        return carry

    lax.fori_loop(0, 2, direct_block, 0)

    def across_block(i, carry):
        d = (i // 2 + 1) % 3 * 3 + i % 2 * 2

        @pl.when(exists(d))
        def _():
            for copy in halo_copies(4, d, d, False):
                copy.wait_recv()
            side_block(d)

        return carry

    lax.fori_loop(0, 6, across_block, 0)

    inner = {-1: [3], 0: [0, 1, 2, 3], 1: [0]}
    for d in directions:

        @pl.when(exists(d))
        def _(d=d):
            even, odd = boxes_of(d, 0)
            for i, r in enumerate(inner[d // 3 - 1]):
                for j, c in enumerate(inner[d % 3 - 1]):
                    place = span(d // 3 - 1)[i] * 6 + span(d % 3 - 1)[j]
                    window[place] = (odd if c % 2 else even)[r * 2 + c // 2]

    def forward_row(r, carry):
        for c in range(4):
            a = jnp.zeros((8, 128), F32)
            b = jnp.zeros((8, 128), F32)
            for k in range(2):
                code = codes[r, k, c]
                place = jnp.where(code == 9, 36, (r + code // 3) * 6 + c + code % 3)
                v = window[place].astype(BF16)
                a += nt(v, near[0, r * 4 + c, k])
                b += nt(v, near[1, r * 4 + c, k])
            near_fwd[r * 4 + c] = a + swap(b)
        return carry

    lax.fori_loop(0, 4, forward_row, 0)

    for d in directions:

        @pl.when(exists(d))
        def _(d=d):
            ring_copy(8 - d).wait_recv()
            at = 0
            rows = {-1: [1], 0: [1, 2, 3, 4], 1: [4]}
            for r in rows[d // 3 - 1]:
                for c in rows[d % 3 - 1]:
                    placed[r * 6 + c] += ring_in[d, at]
                    at += 1

    others = gath.at[pl.ds(0, n_col - 1)]
    pltpu.make_async_copy(others, others, all_recv.at[1]).wait()
    loads[8].wait()

    def coarse_row(rp, carry):
        acc = list(carry)
        ri = row - rp + n_row - 1
        for cp in range(n_col):
            ci = col - cp + n_col - 1
            apart = (jnp.abs(row - rp) > 1) | (jnp.abs(col - cp) > 1)
            weight = jnp.where(apart, 1.0, 0.0)
            values = gath[cp, rp].astype(F32)
            for s in range(2):
                rs = ri if s == 0 else 2 * (n_row - 1) - ri
                cs = ci if s == 0 else 2 * (n_col - 1) - ci
                coeff = coarse_tab[rs, cs].astype(F32)
                t_re = coeff[0:1] * weight
                t_im = coeff[1:2] * (weight if s == 0 else -weight)
                v = values[8 * s : 8 * s + 8]
                acc[2 * s] += t_re * v
                acc[2 * s + 1] += t_im * v
        return tuple(acc)

    sums = lax.fori_loop(0, n_row, coarse_row, (jnp.zeros((8, 256), F32),) * 4)

    for s in range(2):
        arrived = sums[2 * s] + swap(sums[2 * s + 1])
        turned = swap(arrived)
        down = [trig[0, j : j + 1] * arrived - trig[1, j : j + 1] * turned for j in range(16)]
        spread = nn(jnp.concatenate(down, 0), interp[...], HIGH)
        incoming = (leaf[s].reshape(128, 128) + spread).astype(BF16)
        both = nn(incoming, w_rcv[s])
        far = both[:, :128].reshape(16, 8, 128) + swap(both[:, 128:].reshape(16, 8, 128))
        out = out_fwd if s == 0 else out_adj
        for j in range(8):
            pair = []
            for b in (2 * j, 2 * j + 1):
                close = near_fwd[b] if s == 0 else placed[(b // 4 + 1) * 6 + b % 4 + 1]
                pair.append(far[b] + close)
            low = upper((8, 128))
            out[0, j] = jnp.where(low, pair[0], pltpu.roll(pair[1], 4, 0))
            out[1, j] = jnp.where(low, pltpu.roll(pair[0], 4, 0), pair[1])

    for d in directions:

        @pl.when(exists(d))
        def _(d=d):
            for copy in halo_copies(4, d, 8 - d, d % 2 == 1):
                copy.wait_send()
            ring_copy(d).wait_send()

    pltpu.make_async_copy(column, column, all_send.at[0]).wait()
    pltpu.make_async_copy(others, others, all_send.at[1]).wait()


def per_device(
    n_row,
    n_col,
    current,
    probe,
    near_list,
    near_blocks,
    radiation,
    reception,
    interp,
    phase,
    leaf_table,
    coarse_table,
):
    vmem = pl.BlockSpec(memory_space=pltpu.VMEM)
    hbm = pl.BlockSpec(memory_space=pltpu.HBM)
    leaf_rows = jnp.transpose(leaf_table, (1, 2, 0, 3))
    coarse_rows = jnp.transpose(coarse_table, (1, 2, 0, 3))
    half = pltpu.VMEM((2, 8, 8, 128), F32)
    dma = pltpu.SemaphoreType.DMA
    fwd, adj = pl.pallas_call(
        functools.partial(kernel, n_row, n_col),
        out_shape=(half, half),
        in_specs=[hbm, hbm, pl.BlockSpec(memory_space=pltpu.SMEM)] + [hbm] * 7,
        out_specs=(vmem, vmem),
        scratch_shapes=[
            pltpu.VMEM(radiation.shape, BF16),
            pltpu.VMEM(reception.shape, BF16),
            pltpu.VMEM(interp.shape, F32),
            pltpu.VMEM(phase.shape, F32),
            pltpu.VMEM(leaf_rows.shape, F32),
            pltpu.VMEM(coarse_rows.shape, BF16),
            pltpu.VMEM((9, 256, 128), BF16),
            pltpu.VMEM((n_col, n_row, 16, 256), BF16),
            pltpu.VMEM((2, 16, 2, 128, 128), BF16),
            pltpu.VMEM((2, 128, 256), BF16),
            pltpu.VMEM((2, 128, 256), BF16),
            pltpu.VMEM((2, 225, 8, 128), F32),
            pltpu.VMEM((2, 2, 8, 2, 8, 128), F32),
            pltpu.VMEM((2, 16, 8, 128), F32),
            pltpu.VMEM((1, 2, 8, 256), F32),
            pltpu.VMEM((37, 8, 128), F32),
            pltpu.VMEM((36, 8, 128), F32),
            pltpu.VMEM((9, 4, 8, 128), F32),
            pltpu.VMEM((9, 4, 8, 128), F32),
            pltpu.VMEM((16, 8, 128), F32),
            pltpu.VMEM((8, 2, 8, 128), F32),
            pltpu.VMEM((2, 16, 256), F32),
            dma((9,)),
            dma((2, 9)),
            dma((2, 9)),
            dma((9,)),
            dma((9,)),
            dma((2,)),
            dma((2,)),
        ],
        compiler_params=pltpu.CompilerParams(
            collective_id=0, has_side_effects=True, vmem_limit_bytes=63 * 1024 * 1024
        ),
        name="operator",
    )(
        current.reshape(128, 128),
        probe.reshape(128, 128),
        jnp.transpose(near_list, (0, 2, 1)),
        near_blocks.reshape(2, 16, 2, 128, 128),
        radiation,
        reception,
        interp,
        phase,
        leaf_rows,
        coarse_rows,
    )
    return fwd.reshape(current.shape), adj.reshape(current.shape)


def solution(mesh):
    placed = (
        P(None, "row", "col", None, None),
        P(None, "row", "col", None, None),
        P("row", "col", None),
        P(None, "row", "col", None, None, None),
        P(),
        P(),
        P(),
        P(),
        P(),
        P(),
    )
    return jax.shard_map(
        functools.partial(per_device, mesh.shape["row"], mesh.shape["col"]),
        mesh=mesh,
        in_specs=placed,
        out_specs=(P(None, "row", "col", None, None), P(None, "row", "col", None, None)),
        check_vma=False,
    )
```
